256 devices in a mesh: occ: 4 (over x_lo, core), vir: 16 (over z, x_hi), rep: 4 (over y).
Axes of the slice: x: 4 (x_hi: 2, x_lo: 2; x = x_hi * 2 + x_lo), y: 4, z: 8, core: 2. Of those that a mesh axis runs over, the one named last changes fastest.
Arguments:
- integrals: float32 [8192, 16384], P('vir', 'rep'), may hold values from -0.046875 to 0.046875
- amplitudes: float32 [16384, 4096], P(('rep', 'vir'), 'occ'), may hold values from -6 to 6
Outputs:
- ladder: float32 [8192, 4096], P('vir', ('occ', 'rep'))
The draws below stay inside these ranges and needn't reach their ends.
All inputs are finite; a program needn't handle non-finite values.
Results may differ from the reference program's by a relative error of at most 0.00007.
Values sent between devices are 32-bit elements; how exact they have to be, the bound alone decides.
No kernel may reach another device: no remote copies, remote signals or barrier semaphores. Data moves between devices by JAX's collectives and lax.ppermute only.
A program may use at most 128 MiB of HBM per device.

```python
import jax
import jax.numpy as jnp
from jax import lax

O = 64
KCD = 16384
PAB = 8192
NIJ = 4096


def level_of(rng, dims, shards, least, largest):
    level = 1.0
    for axis_at, parts in shards:
        steps = jax.random.uniform(jax.random.fold_in(jax.random.fold_in(rng, 6), axis_at), (parts,), jnp.float32, least / len(shards), largest / len(shards))
        level = level * jnp.repeat(jnp.exp(steps), dims[axis_at] // parts).reshape((-1,) + (1,) * (len(dims) - 1 - axis_at))
    return level


def noise(rng, extent, deviation, limit, split=(), kind=jnp.bfloat16):
    values = deviation * jax.random.normal(rng, extent, jnp.float32)
    if split:
        values = values * level_of(rng, extent, split, -0.22, 0.18)
    return jnp.clip(values, -limit, limit).astype(kind)


def setup_inputs(seed: int = 0) -> dict:
    streams_of = jax.random.split(jax.random.key(seed), 3)
    return {
        "integrals": noise(streams_of[0], (PAB, KCD), KCD ** -0.5, 0.046875, ((0, 16), (1, 4)), jnp.float32),
        "amplitudes": noise(streams_of[1], (KCD, NIJ), 1.0, 6.0, ((0, 64), (1, 4)), jnp.float32),
    }


def reference(integrals, amplitudes):
    raw = jnp.dot(integrals, amplitudes, preferred_element_type=jnp.float32, precision=lax.Precision.HIGHEST)
    middle = PAB // 2
    mirror = jnp.concatenate([raw[middle:], raw[:middle]], axis=0)
    paired = raw - mirror
    cube = paired.reshape(PAB, O, O)
    ladder = cube - jnp.transpose(cube, (0, 2, 1))
    return ladder.reshape(PAB, NIJ)
```

```python
import functools

import jax
import jax.numpy as jnp
import numpy as np
from jax import lax
from jax.experimental import pallas as pl
from jax.experimental.pallas import tpu as pltpu
from jax.sharding import Mesh, PartitionSpec as P

O = 64
GROUP = ("xl", "c", "y")
F32, BF16 = jnp.float32, jnp.bfloat16


def quad_partners(o, a, p):
    return (a, a ^ 2) if o < (o ^ p) else (a ^ 1, a ^ 3)


def own_pairs(o, a):
    g = 4 * o + a
    h = 4 * o + (a + 1) % 4
    out = [(4 * g + s, 4 * h + t) for s in range(4) for t in range(4)]
    h = 4 * o + (a ^ 2)
    if a < (a ^ 2):
        out += [(4 * g + s, 4 * h + t) for s in (0, 1) for t in range(4)]
    else:
        out += [(4 * g + s, 4 * h + t) for t in (2, 3) for s in range(4)]
    out += [(4 * g + s, 4 * g + t) for s in range(4) for t in range(s + 1, 4)]
    out += [None, None]
    lists = [out]
    for p in (1, 2, 3):
        lists.append([(4 * g + s, 4 * (4 * (o ^ p) + b) + t) for b in quad_partners(o, a, p) for s in range(4) for t in range(4)])
    return lists


def select_table():
    table = -np.ones((4, 2, 896), np.int32)
    for o in range(4):
        for a in range(4):
            for p, pairs in enumerate(own_pairs(o, a)):
                for k, pair in enumerate(pairs):
                    if pair is None:
                        continue
                    i, j = pair
                    at = p * 128 + a * 32 + k
                    table[o, 0, at] = (i - 16 * o) * O + j
                    if p == 0:
                        table[o, 1, at] = (j - 16 * o) * O + i
            for p in (1, 2, 3):
                for k, (j, i) in enumerate(own_pairs(o ^ p, a)[p]):
                    table[o, 0, 512 + (p - 1) * 128 + a * 32 + k] = (i - 16 * o) * O + j
    return table


def send_perms():
    quads = [(o, a) for o in range(4) for a in range(4)]
    perms = [
        (range(0, 16), [(4 * o + a, 4 * o + (a + 1) % 4) for o, a in quads]),
        (range(16, 24), [(4 * o + a, 4 * o + (a ^ 2)) for o, a in quads]),
    ]
    for p in (1, 2, 3):
        for t in (0, 1):
            start = 32 * p + 16 * t
            perms.append((range(start, start + 16), [(4 * o + a, 4 * (o ^ p) + quad_partners(o, a, p)[t]) for o, a in quads]))
    return perms


def expand_table():
    own = [sum(own_pairs(g // 4, g % 4), []) for g in range(16)]
    table = np.zeros((16, 2, 256), np.int32)
    table[:, 0] = -1
    held = [list(own[g]) for g in range(16)]
    for slots, perm in send_perms():
        for source, target in perm:
            held[target] += [own[source][s] for s in slots]
    for g in range(16):
        for slot, pair in enumerate(held[g]):
            if pair is None:
                continue
            for (i, j), sign in ((pair, 1), (pair[::-1], -1)):
                if i // 4 == g:
                    table[g, :, (i - 4 * g) * O + j] = slot, sign
        assert sum(table[g, 0] < 0) == 4
    return table


def parts_of(x, n):
    parts = []
    for _ in range(n):
        part = x.astype(BF16)
        parts.append(part)
        x = x - part.astype(F32)
    return parts


def call(body, out, *args, scratch=(), flops=0, smem=(), moved=None, vmem=48 * 2**20):
    in_specs = [pl.BlockSpec(memory_space=pltpu.SMEM if k in smem else pltpu.VMEM) for k in range(len(args))]
    if moved is None:
        moved = sum(4 * a.size for a in args) + sum(4 * int(np.prod(s.shape)) for s in out)
    return pl.pallas_call(
        body,
        out_shape=out,
        in_specs=in_specs,
        out_specs=[pl.BlockSpec(memory_space=pltpu.VMEM)] * len(out),
        scratch_shapes=list(scratch),
        compiler_params=pltpu.CompilerParams(vmem_limit_bytes=vmem),
        cost_estimate=pl.CostEstimate(flops=flops, bytes_accessed=moved, transcendentals=0),
    )(*args)


def f32(*shape):
    return jax.ShapeDtypeStruct(shape, F32)


def select_body(table_ref, b_ref, *outs):
    kept01, kept23, sent1, sent2, sent3 = outs
    parts = parts_of(b_ref[...], 3)
    for n, (ref, lo, p) in enumerate([
        (sent1, 0, 4), (sent2, 0, 5), (sent3, 0, 6), (kept01, 0, 0), (kept01, 128, 1), (kept23, 0, 2), (kept23, 128, 3)]):
        cols = slice(p * 128, p * 128 + 128)
        row = lax.broadcasted_iota(jnp.int32, (b_ref.shape[1], 128), 0)
        hot = jnp.where(row == table_ref[0:1, cols], 1.0, 0.0)
        if p == 0:
            hot = hot - jnp.where(row == table_ref[1:2, cols], 1.0, 0.0)
        hot = hot.astype(BF16)
        acc = jnp.dot(parts[0], hot, preferred_element_type=F32)
        for part in parts[1:]:
            acc += jnp.dot(part, hot, preferred_element_type=F32)
        ref[:, lo:lo + 128] = acc


def sub_body(x_ref, *refs):
    o_ref = refs[-1]
    width = x_ref.shape[1]
    first = width - 128 * (len(refs) - 1)
    if first:
        o_ref[:, :first] = x_ref[:, :first]
    for k, ref in enumerate(refs[:-1]):
        at = slice(first + 128 * k, first + 128 * k + 128)
        o_ref[:, at] = x_ref[:, at] - ref[...]


def give_body(index_ref, a_ref, o_ref):
    o_ref[...] = a_ref[...]


def split_body(index_ref, a_ref, hi_ref, lo_ref):
    hi_ref[...], lo_ref[...] = parts_of(a_ref[...], 2)


def split_rows_body(q_ref, *refs):
    hi_ref, lo_ref = refs[-2:]
    half = hi_ref.shape[1] // 2
    for n in range(4):
        rows = pl.ds(pl.multiple_of((q_ref[0] ^ n) * 128, 128), 128)
        for k in range(2):
            hi, lo = parts_of(refs[2 * n + k][...], 2)
            hi_ref[rows, k * half:(k + 1) * half] = hi
            lo_ref[rows, k * half:(k + 1) * half] = lo


def runs_of(positions):
    runs = []
    for n, at in enumerate(positions):
        if runs and runs[-1][0] + runs[-1][2] == at:
            runs[-1][2] += 1
        else:
            runs.append([at, n, 1])
    return runs


def product_body(positions, has_total, last, *refs):
    refs = list(refs)
    y_ref = refs.pop(0)
    a_refs = [refs.pop(0) for _ in range(4)]
    blocks = [refs.pop(0) for _ in positions]
    before = refs.pop(0) if has_total else None
    outs = [refs.pop(0) for _ in range(4 if last else 1)]
    bh, bl = refs.pop(0), refs.pop(0)
    turned = refs.pop(0) if last else None
    depth = blocks[0].shape[0]
    for n, block in enumerate(blocks):
        bh[n * depth:(n + 1) * depth, :], bl[n * depth:(n + 1) * depth, :] = parts_of(block[...], 2)
    height = 256
    for half in range(2):
        ah, al = a_refs[2 * half:2 * half + 2]
        for m in range(ah.shape[0] // height):
            rows = slice(m * height, (m + 1) * height)
            at = half * ah.shape[0] + m * height
            total = before[at:at + height, :] if has_total else None
            for position, n, count in runs_of(positions):
                cols = slice(position * depth, (position + count) * depth)
                of = slice(n * depth, (n + count) * depth)
                for a, b in ((ah, bh), (al, bh), (ah, bl)):
                    term = jnp.dot(a[rows, cols], b[of, :], preferred_element_type=F32)
                    total = term if total is None else total + term
            if last:
                turned[:, at:at + height] = total.T
            else:
                outs[0][at:at + height, :] = total
    if last:
        for r in range(4):
            first = ((y_ref[0] + r) % 4) * 32
            outs[r][0:32, :] = turned[pl.ds(pl.multiple_of(first, 32), 32), :]
            outs[r][32:64, :] = turned[pl.ds(pl.multiple_of(first + 128, 32), 32), :]


def sum_body(a, b, c, d, keep, give):
    rows = keep.shape[1]
    keep[...] = (a[:, :rows] + b[:, :rows]) + (c[:, :rows] + d[:, :rows])
    give[...] = (a[:, rows:] + b[:, rows:]) + (c[:, rows:] + d[:, rows:])


def add_body(a, b, o):
    o[...] = a[...] + b[...]


def pair_body(cuts, a, b, o, *sends):
    value = a[...] - b[...]
    o[...] = value
    for (first, count), ref in zip(cuts, sends):
        ref[...] = value[first:first + count, :]


def expand_body(table_ref, *refs):
    *ins, o_ref, held = refs
    at = 0
    for ref in ins:
        held[at:at + ref.shape[0], :] = ref[...]
        at += ref.shape[0]
    held[at:, :] = jnp.zeros((held.shape[0] - at, held.shape[1]), F32)
    row = lax.broadcasted_iota(jnp.int32, (held.shape[0], o_ref.shape[1]), 0)
    hot = jnp.where(row == table_ref[0:1, :], table_ref[1:2, :].astype(F32), 0.0).astype(BF16)
    turned = held[...].T
    acc = None
    for part in parts_of(turned, 3):
        term = jnp.dot(part, hot, preferred_element_type=F32)
        acc = term if acc is None else acc + term
    o_ref[...] = acc


def moved_along(value, axis, step):
    n = lax.axis_size(axis)
    return lax.ppermute(value, axis, [(k, (k + step) % n) for k in range(n)])


def flipped(value, axes, mask):
    n = lax.axis_size(axes)
    return lax.ppermute(value, axes, [(k, k ^ mask) for k in range(n)])


def blocks_of_a(body, index, a, height, row_at, outs, dtype):
    depth = a.shape[1] // 16
    spec = pltpu.PrefetchScalarGridSpec(
        num_scalar_prefetch=1,
        grid=(8,),
        in_specs=[pl.BlockSpec((height, depth), lambda d, index: (index[8] if row_at else 0, index[d]))],
        out_specs=[pl.BlockSpec((height, depth), lambda d, index: (0, d))] * outs,
    )
    return pl.pallas_call(
        body,
        grid_spec=spec,
        out_shape=[jax.ShapeDtypeStruct((height, 8 * depth), dtype)] * outs,
        cost_estimate=pl.CostEstimate(flops=0, bytes_accessed=height * depth * 8 * 8, transcendentals=0),
    )(index, a)


def shards(integrals, amplitudes):
    xl, c, z, xh, y = (lax.axis_index(n) for n in ("xl", "c", "z", "xh", "y"))
    occ = 2 * xl + c
    select = lax.dynamic_index_in_dim(jnp.asarray(select_table()), occ, 0, False)
    expand = lax.dynamic_index_in_dim(jnp.asarray(expand_table()), 4 * occ + y, 0, False)
    ring = 2 * ((z + jnp.arange(8, dtype=jnp.int32)) % 8)

    k = amplitudes.shape[0]
    kept01, kept23, sent1, sent2, sent3 = call(
        select_body, [f32(k, 256), f32(k, 256), f32(k, 128), f32(k, 128), f32(k, 128)],
        select, amplitudes, flops=2 * k * 1024 * 896 * 3)
    (first,) = call(sub_body, [f32(k, 256)], kept01, flipped(sent1, ("xl", "c"), 1))
    (second,) = call(sub_body, [f32(k, 256)], kept23, flipped(sent2, ("xl", "c"), 2), flipped(sent3, ("xl", "c"), 3))

    quarter_out = 2 * (1 - xl) + c
    index = jnp.concatenate([ring + (1 - xh), quarter_out[None]])
    (give,) = blocks_of_a(give_body, index, integrals, 128, True, 1, F32)
    half = give.shape[1] // 2
    quarters = [[], [], [], []]
    for n in range(2):
        piece = flipped(give[:, n * half:(n + 1) * half], ("xl", "xh"), 3)
        beside = flipped(piece, ("xl",), 1)
        for q, value in enumerate((piece, flipped(piece, ("c",), 1), beside, flipped(beside, ("c",), 1))):
            quarters[q].append(value)
    own_hi, own_lo = blocks_of_a(split_body, jnp.concatenate([ring + xh, quarter_out[None]]), integrals, 512, False, 2, BF16)
    wide = jax.ShapeDtypeStruct((512, 2 * half), BF16)
    other_hi, other_lo = call(split_rows_body, [wide, wide], occ[None], *sum(quarters, []), smem=(0,))

    a = (own_hi, own_lo, other_hi, other_lo)

    def product(blocks, positions, total, last):
        args = (y[None], *a, *blocks) + ((total,) if total is not None else ())
        n = len(blocks)
        out = [f32(64, 1024)] * 4 if last else [f32(1024, 256)]
        scratch = [pltpu.VMEM((n * k, 256), BF16)] * 2 + ([pltpu.VMEM((256, 1024), F32)] if last else [])
        return call(functools.partial(product_body, positions, total is not None, last), out, *args,
                    scratch=scratch, smem=(0,), flops=2 * 1024 * 256 * n * k * 3)

    def reduced(pieces):
        arrived = [moved_along(pieces[r], "y", r) for r in (1, 2, 3)]
        keep, give = call(sum_body, [f32(64, 512)] * 2, pieces[0], *arrived)
        (mine,) = call(add_body, [f32(64, 512)], keep, flipped(give, ("xh",), 1))
        return mine, moved_along(mine, "z", 4)

    chunks = []
    for block, ups in ((first, 4), (second, 3)):
        held = {0: block}
        up = down = block
        for step in range(1, 5):
            if step <= ups:
                up = moved_along(up, "z", 1)
                held[(8 - step) % 8] = up
            if step <= 7 - ups:
                down = moved_along(down, "z", -1)
                held[step] = down
        chunks.append(held)

    held = chunks[0]
    pieces = product([held[d] for d in range(8)], tuple(range(8)), None, True)
    mine0, mirror0 = reduced(pieces)
    held = chunks[1]
    early, late = (0, 1, 2, 6, 7), (3, 4, 5)
    (total,) = product([held[d] for d in early], early, None, False)
    pieces = product([held[d] for d in late], late, total, True)
    mine1, mirror1 = reduced(pieces)

    perms = send_perms()
    cuts = [(s[0], len(s)) for s, _ in perms]
    pair0, *sends0 = call(functools.partial(pair_body, cuts[:4]), [f32(64, 512)] + [f32(n, 512) for _, n in cuts[:4]], mine0, mirror0)
    cuts1 = [(first - 64, n) for first, n in cuts[4:]]
    pair1, *sends1 = call(functools.partial(pair_body, cuts1), [f32(64, 512)] + [f32(n, 512) for _, n in cuts1], mine1, mirror1)
    arrived = [lax.ppermute(value, GROUP, perm) for value, (_, perm) in zip(sends0 + sends1, perms)]
    (ladder,) = call(expand_body, [f32(512, 256)], expand, pair0, pair1, *arrived,
                     scratch=[pltpu.VMEM((256, 512), F32)], flops=2 * 512 * 256 * 256 * 3)
    return ladder


def solution(mesh):
    fine = Mesh(mesh.devices.reshape(2, 2, 8, 2, 4), ("xl", "c", "z", "xh", "y"))
    in_specs = (P(("z", "xh"), "y"), P(("y", "z", "xh"), ("xl", "c")))
    out_specs = P(("z", "xh"), ("xl", "c", "y"))
    return jax.shard_map(shards, mesh=fine, in_specs=in_specs, out_specs=out_specs, check_vma=False)
```

```python
import functools

import jax
import jax.numpy as jnp
import numpy as np
from jax import lax
from jax.experimental import pallas as pl
from jax.experimental.pallas import tpu as pltpu
from jax.sharding import Mesh, PartitionSpec as P

O = 64
GROUP = ("xl", "c", "y")
F32, BF16 = jnp.float32, jnp.bfloat16
VMEM_PRODUCT = 57 * 2**20


def quad_partners(o, a, p):
    return (a, a ^ 2) if o < (o ^ p) else (a ^ 1, a ^ 3)


def own_pairs(o, a):
    g = 4 * o + a
    h = 4 * o + (a + 1) % 4
    out = [(4 * g + s, 4 * h + t) for s in range(4) for t in range(4)]
    h = 4 * o + (a ^ 2)
    if a < (a ^ 2):
        out += [(4 * g + s, 4 * h + t) for s in (0, 1) for t in range(4)]
    else:
        out += [(4 * g + s, 4 * h + t) for t in (2, 3) for s in range(4)]
    out += [(4 * g + s, 4 * g + t) for s in range(4) for t in range(s + 1, 4)]
    out += [None, None]
    lists = [out]
    for p in (1, 2, 3):
        lists.append([(4 * g + s, 4 * (4 * (o ^ p) + b) + t) for b in quad_partners(o, a, p) for s in range(4) for t in range(4)])
    return lists


def select_table():
    table = -np.ones((4, 2, 896), np.int32)
    for o in range(4):
        for a in range(4):
            for p, pairs in enumerate(own_pairs(o, a)):
                for k, pair in enumerate(pairs):
                    if pair is None:
                        continue
                    i, j = pair
                    at = p * 128 + a * 32 + k
                    table[o, 0, at] = (i - 16 * o) * O + j
                    if p == 0:
                        table[o, 1, at] = (j - 16 * o) * O + i
            for p in (1, 2, 3):
                for k, (j, i) in enumerate(own_pairs(o ^ p, a)[p]):
                    table[o, 0, 512 + (p - 1) * 128 + a * 32 + k] = (i - 16 * o) * O + j
    return table


def send_perms():
    quads = [(o, a) for o in range(4) for a in range(4)]
    perms = [
        (range(0, 16), [(4 * o + a, 4 * o + (a + 1) % 4) for o, a in quads]),
        (range(16, 24), [(4 * o + a, 4 * o + (a ^ 2)) for o, a in quads]),
    ]
    for p in (1, 2, 3):
        for t in (0, 1):
            start = 32 * p + 16 * t
            perms.append((range(start, start + 16), [(4 * o + a, 4 * (o ^ p) + quad_partners(o, a, p)[t]) for o, a in quads]))
    return perms


def expand_table():
    own = [sum(own_pairs(g // 4, g % 4), []) for g in range(16)]
    table = np.zeros((16, 2, 256), np.int32)
    table[:, 0] = -1
    held = [list(own[g]) for g in range(16)]
    for slots, perm in send_perms():
        for source, target in perm:
            held[target] += [own[source][s] for s in slots]
    for g in range(16):
        for slot, pair in enumerate(held[g]):
            if pair is None:
                continue
            for (i, j), sign in ((pair, 1), (pair[::-1], -1)):
                if i // 4 == g:
                    table[g, :, (i - 4 * g) * O + j] = slot, sign
        assert sum(table[g, 0] < 0) == 4
    return table


def parts_of(x, n):
    parts = []
    for _ in range(n):
        part = x.astype(BF16)
        parts.append(part)
        x = x - part.astype(F32)
    return parts


def call(body, out, *args, scratch=(), smem=(), vmem=16 * 2**20, anywhere=(), after=(), flops=0):
    spaces = [pltpu.SMEM if k in smem else pl.ANY if k in anywhere else pltpu.VMEM for k in range(len(args))]
    count = len(args)

    def without_after(*refs):
        body(*refs[:count], *refs[count + len(after):])

    return pl.pallas_call(
        without_after,
        out_shape=out,
        in_specs=[pl.BlockSpec(memory_space=m) for m in spaces + [pl.ANY] * len(after)],
        out_specs=[pl.BlockSpec(memory_space=pltpu.VMEM)] * len(out),
        scratch_shapes=list(scratch),
        compiler_params=pltpu.CompilerParams(vmem_limit_bytes=vmem),
        cost_estimate=pl.CostEstimate(flops=flops, bytes_accessed=0, transcendentals=0),
    )(*args, *after)


def in_step(value, after):
    def body(source, target):
        target[...] = source[...]

    return call(body, [jax.ShapeDtypeStruct(value.shape, value.dtype)], value, after=after)[0]


def f32(*shape):
    return jax.ShapeDtypeStruct(shape, F32)


def select_body(occ_ref, table_ref, b_ref, *outs):
    kept, sent1, sent2, sent3 = outs
    parts = parts_of(b_ref[...], 2)
    for n, (ref, lo, p) in enumerate([
        (sent1, 0, 4), (sent2, 0, 5), (sent3, 0, 6), (kept, 0, 0), (kept, 128, 1), (kept, 256, 2), (kept, 384, 3)]):
        cols = slice(p * 128, p * 128 + 128)
        row = lax.broadcasted_iota(jnp.int32, (b_ref.shape[1], 128), 0)
        hot = jnp.where(row == table_ref[occ_ref[0], 0:1, cols], 1.0, 0.0)
        if p == 0:
            hot = hot - jnp.where(row == table_ref[occ_ref[0], 1:2, cols], 1.0, 0.0)
        hot = hot.astype(BF16)
        acc = jnp.dot(parts[0], hot, preferred_element_type=F32)
        for part in parts[1:]:
            acc += jnp.dot(part, hot, preferred_element_type=F32)
        ref[:, lo:lo + 128] = acc


def sub_body(x_ref, *refs):
    o_ref = refs[-1]
    width = x_ref.shape[1]
    first = width - 128 * (len(refs) - 1)
    if first:
        o_ref[:, :first] = x_ref[:, :first]
    for k, ref in enumerate(refs[:-1]):
        at = slice(first + 128 * k, first + 128 * k + 128)
        o_ref[:, at] = x_ref[:, at] - ref[...]


def product_body(places, has_total, last, at_ref, a_ref, *refs):
    refs = list(refs)
    blocks = [refs.pop(0) for _ in places]
    before = refs.pop(0) if has_total else None
    outs = [refs.pop(0) for _ in range(8 if last else 1)]
    held, sems, a_parts, b_parts, turned = refs
    depth, width = blocks[0].shape
    copies = []
    for n, (up, other) in enumerate(places):
        block = 2 * ((at_ref[1] + up) % 8) + (at_ref[2] + other) % 2
        cols = pl.ds(pl.multiple_of(block * depth, depth), depth)
        copies.append(pltpu.make_async_copy(a_ref.at[:, cols], held.at[n], sems.at[n]))
        copies[-1].start()
    for n, block in enumerate(blocks):
        hi, lo = parts_of(block[...], 2)
        for m, part in enumerate((hi, hi, lo)):
            b_parts[(3 * n + m) * depth:(3 * n + m + 1) * depth, :] = part
    for n, copy in enumerate(copies):
        copy.wait()
        hi, lo = parts_of(held[n], 2)
        for m, part in enumerate((hi, lo, hi)):
            a_parts[:, (3 * n + m) * depth:(3 * n + m + 1) * depth] = part
    tile = 256
    for m in range(held.shape[1] // tile):
        rows = slice(m * tile, (m + 1) * tile)
        for n in range(width // tile):
            cols = slice(n * tile, (n + 1) * tile)
            total = jnp.dot(a_parts[rows, :], b_parts[:, cols], preferred_element_type=F32)
            if has_total:
                total += before[rows, cols]
            if last:
                turned[cols, rows] = total.T
            else:
                outs[0][rows, cols] = total
    if last:
        for r in range(4):
            first = ((at_ref[0] + r) % 4) * 32
            for p in range(4):
                outs[r + p // 2 * 4][p % 2 * 32:p % 2 * 32 + 32, :] = turned[pl.ds(pl.multiple_of(p * 128 + first, 32), 32), :]


def sum_body(a, b, c, d, o):
    o[...] = (a[...] + b[...]) + (c[...] + d[...])


def pair_body(cuts, a, b, o, *sends):
    value = a[...] - b[...]
    o[...] = value
    for (first, count), ref in zip(cuts, sends):
        ref[...] = value[first:first + count, :]


def expand_body(quad_ref, table_ref, *refs):
    *ins, o_ref, held = refs
    at = 0
    for ref in ins:
        held[at:at + ref.shape[0], :] = ref[...]
        at += ref.shape[0]
    held[at:, :] = jnp.zeros((held.shape[0] - at, held.shape[1]), F32)
    row = lax.broadcasted_iota(jnp.int32, (held.shape[0], o_ref.shape[1]), 0)
    table = table_ref[quad_ref[0]]
    hot = jnp.where(row == table[0:1, :], table[1:2, :].astype(F32), 0.0).astype(BF16)
    turned = held[...].T
    acc = None
    for part in parts_of(turned, 3):
        term = jnp.dot(part, hot, preferred_element_type=F32)
        acc = term if acc is None else acc + term
    o_ref[...] = acc


def moved_along(value, axis, step):
    n = lax.axis_size(axis)
    return lax.ppermute(value, axis, [(k, (k + step) % n) for k in range(n)])


def flipped(value, axes, mask):
    n = lax.axis_size(axes)
    return lax.ppermute(value, axes, [(k, k ^ mask) for k in range(n)])


STEPS = (
    ((0, 0), (0, 0), (0, 0)),
    ((-1, 0), (1, 0), (1, 0)),
    ((-2, 0), (2, 0), (2, 0)),
    ((-3, 0), (2, 1), (-2, 0)),
    ((-2, 1), (3, 1), (-1, 0)),
)


def gather_step(held, step):
    up, down, across = STEPS[step]
    held[up[0] - 1, up[1]] = moved_along(held[up], "z", 1)
    held[down[0] + 1, down[1]] = moved_along(held[down], "z", -1)
    held[across[0], 1] = flipped(held[across], "xh", 1)
    return (up[0] - 1, up[1]), (down[0] + 1, down[1]), (across[0], 1)


def shards(integrals, amplitudes):
    xl, c, z, xh, y = (lax.axis_index(n) for n in ("xl", "c", "z", "xh", "y"))
    occ = 2 * xl + c
    quad = (4 * occ + y)[None]
    at = jnp.stack([y, z, xh])

    k = amplitudes.shape[0]
    kept, sent1, sent2, sent3 = call(
        select_body, [f32(k, 512), f32(k, 128), f32(k, 128), f32(k, 128)],
        occ[None], jnp.asarray(select_table()), amplitudes, smem=(0,))
    arrived = [flipped(value, ("xl", "c"), p) for p, value in ((1, sent1), (2, sent2), (3, sent3))]
    (unique,) = call(sub_body, [f32(k, 512)], kept, *arrived)

    def product(held, places, total, last):
        n = len(places)
        args = (at, integrals, *[held[p] for p in places]) + ((total,) if total is not None else ())
        out = [f32(64, 512)] * 8 if last else [f32(512, 512)]
        return call(functools.partial(product_body, places, total is not None, last), out, *args, smem=(0,), anywhere=(1,),
                    scratch=[pltpu.VMEM((n, 512, k), F32), pltpu.SemaphoreType.DMA((n,)), pltpu.VMEM((512, 3 * n * k), BF16),
                             pltpu.VMEM((3 * n * k, 512), BF16), pltpu.VMEM((512, 512), F32)],
                    vmem=VMEM_PRODUCT, flops=2 * 512 * n * k * 512 * 3)

    held = {(0, 0): unique}
    places, total = [(0, 0)], None
    ready = ()
    for step in range(5):
        down = STEPS[step][1]
        if step:
            held[down] = in_step(held[down], ready)
        arrived = gather_step(held, step)
        ready = (held[arrived[2]],)
        if step:
            (total,) = product(held, tuple(places), total, False)
            ready += (total,)
            places = []
        places += arrived
    total = product(held, tuple(places), total, True)

    perms = send_perms()
    pairs, arrived = [], []
    for n, pieces in enumerate((total[:4], total[4:])):
        moved = [moved_along(pieces[r], "y", r) for r in (1, 2, 3)]
        (mine,) = call(sum_body, [f32(64, 512)], pieces[0], *moved)
        lots = perms[4 * n:4 * n + 4]
        cuts = [(slots[0] - 64 * n, len(slots)) for slots, _ in lots]
        pair, *sends = call(functools.partial(pair_body, cuts), [f32(64, 512)] + [f32(count, 512) for _, count in cuts],
                            mine, moved_along(mine, "z", 4))
        pairs.append(pair)
        arrived += [lax.ppermute(value, GROUP, perm) for value, (_, perm) in zip(sends, lots)]
    (ladder,) = call(expand_body, [f32(512, 256)], quad, jnp.asarray(expand_table()), *pairs, *arrived,
                     scratch=[pltpu.VMEM((256, 512), F32)], smem=(0,))
    return ladder


def solution(mesh):
    fine = Mesh(mesh.devices.reshape(2, 2, 8, 2, 4), ("xl", "c", "z", "xh", "y"))
    in_specs = (P(("z", "xh"), "y"), P(("y", "z", "xh"), ("xl", "c")))
    out_specs = P(("z", "xh"), ("xl", "c", "y"))
    return jax.shard_map(shards, mesh=fine, in_specs=in_specs, out_specs=out_specs, check_vma=False)
```

```python
import functools

import jax
import jax.numpy as jnp
import numpy as np
from jax import lax
from jax.experimental import pallas as pl
from jax.experimental.pallas import tpu as pltpu
from jax.sharding import Mesh, PartitionSpec as P

O = 64
GROUP = ("xl", "c", "y")
F32, BF16 = jnp.float32, jnp.bfloat16
VMEM_PRODUCT = 50 * 2**20


def quad_partners(o, a, p):
    return (a, a ^ 2) if o < (o ^ p) else (a ^ 1, a ^ 3)


def own_pairs(o, a):
    g = 4 * o + a
    h = 4 * o + (a + 1) % 4
    out = [(4 * g + s, 4 * h + t) for s in range(4) for t in range(4)]
    h = 4 * o + (a ^ 2)
    if a < (a ^ 2):
        out += [(4 * g + s, 4 * h + t) for s in (0, 1) for t in range(4)]
    else:
        out += [(4 * g + s, 4 * h + t) for t in (2, 3) for s in range(4)]
    out += [(4 * g + s, 4 * g + t) for s in range(4) for t in range(s + 1, 4)]
    out += [None, None]
    lists = [out]
    for p in (1, 2, 3):
        lists.append([(4 * g + s, 4 * (4 * (o ^ p) + b) + t) for b in quad_partners(o, a, p) for s in range(4) for t in range(4)])
    return lists


def select_table():
    table = -np.ones((4, 2, 896), np.int32)
    for o in range(4):
        for a in range(4):
            for p, pairs in enumerate(own_pairs(o, a)):
                for k, pair in enumerate(pairs):
                    if pair is None:
                        continue
                    i, j = pair
                    at = p * 128 + a * 32 + k
                    table[o, 0, at] = (i - 16 * o) * O + j
                    if p == 0:
                        table[o, 1, at] = (j - 16 * o) * O + i
            for p in (1, 2, 3):
                for k, (j, i) in enumerate(own_pairs(o ^ p, a)[p]):
                    table[o, 0, 512 + (p - 1) * 128 + a * 32 + k] = (i - 16 * o) * O + j
    return table


def send_perms():
    quads = [(o, a) for o in range(4) for a in range(4)]
    perms = [
        (range(0, 16), [(4 * o + a, 4 * o + (a + 1) % 4) for o, a in quads]),
        (range(16, 24), [(4 * o + a, 4 * o + (a ^ 2)) for o, a in quads]),
    ]
    for p in (1, 2, 3):
        for t in (0, 1):
            start = 32 * p + 16 * t
            perms.append((range(start, start + 16), [(4 * o + a, 4 * (o ^ p) + quad_partners(o, a, p)[t]) for o, a in quads]))
    return perms


def expand_table():
    own = [sum(own_pairs(g // 4, g % 4), []) for g in range(16)]
    table = np.zeros((16, 2, 256), np.int32)
    table[:, 0] = -1
    held = [list(own[g]) for g in range(16)]
    for slots, perm in send_perms():
        for source, target in perm:
            held[target] += [own[source][s] for s in slots]
    for g in range(16):
        for slot, pair in enumerate(held[g]):
            if pair is None:
                continue
            for (i, j), sign in ((pair, 1), (pair[::-1], -1)):
                if i // 4 == g:
                    table[g, :, (i - 4 * g) * O + j] = slot, sign
        assert sum(table[g, 0] < 0) == 4
    return table


def parts_of(x, n):
    parts = []
    for _ in range(n):
        part = x.astype(BF16)
        parts.append(part)
        x = x - part.astype(F32)
    return parts


def call(body, out, *args, scratch=(), smem=(), vmem=16 * 2**20, anywhere=(), after=(), flops=0):
    spaces = [pltpu.SMEM if k in smem else pl.ANY if k in anywhere else pltpu.VMEM for k in range(len(args))]
    count = len(args)

    def without_after(*refs):
        body(*refs[:count], *refs[count + len(after):])

    return pl.pallas_call(
        without_after,
        out_shape=out,
        in_specs=[pl.BlockSpec(memory_space=m) for m in spaces + [pl.ANY] * len(after)],
        out_specs=[pl.BlockSpec(memory_space=pltpu.VMEM)] * len(out),
        scratch_shapes=list(scratch),
        compiler_params=pltpu.CompilerParams(vmem_limit_bytes=vmem),
        cost_estimate=pl.CostEstimate(flops=flops, bytes_accessed=0, transcendentals=0),
    )(*args, *after)


def in_step(turns, *arrays, after=()):
    count = len(arrays)

    def body(*refs):
        refs = refs[len(turns):]
        for source, target in zip(refs[:count], refs[count:]):
            target[...] = source[...]

    return call(body, [jax.ShapeDtypeStruct(a.shape, a.dtype) for a in arrays], *turns, *arrays, after=after)


def f32(*shape):
    return jax.ShapeDtypeStruct(shape, F32)


def select_body(occ_ref, table_ref, b_ref, *outs):
    kept, sent1, sent2, sent3 = outs
    parts = parts_of(b_ref[...], 2)
    for n, (ref, lo, p) in enumerate([
        (sent1, 0, 4), (sent2, 0, 5), (sent3, 0, 6), (kept, 0, 0), (kept, 128, 1), (kept, 256, 2), (kept, 384, 3)]):
        cols = slice(p * 128, p * 128 + 128)
        row = lax.broadcasted_iota(jnp.int32, (b_ref.shape[1], 128), 0)
        hot = jnp.where(row == table_ref[occ_ref[0], 0:1, cols], 1.0, 0.0)
        if p == 0:
            hot = hot - jnp.where(row == table_ref[occ_ref[0], 1:2, cols], 1.0, 0.0)
        hot = hot.astype(BF16)
        acc = jnp.dot(parts[0], hot, preferred_element_type=F32)
        for part in parts[1:]:
            acc += jnp.dot(part, hot, preferred_element_type=F32)
        ref[:, lo:lo + 128] = acc


def sub_body(x_ref, *refs):
    o_ref = refs[-1]
    width = x_ref.shape[1]
    first = width - 128 * (len(refs) - 1)
    if first:
        o_ref[:, :first] = x_ref[:, :first]
    for k, ref in enumerate(refs[:-1]):
        at = slice(first + 128 * k, first + 128 * k + 128)
        o_ref[:, at] = x_ref[:, at] - ref[...]


def product_body(places, has_total, last, at_ref, a_ref, *refs):
    refs = list(refs)
    blocks = [refs.pop(0) for _ in places]
    before = refs.pop(0) if has_total else None
    outs = [refs.pop(0) for _ in range(8 if last else 1)]
    if not last:
        turn = refs.pop(0)
        turn[...] = jnp.zeros_like(turn)
    held, sems, a_parts, b_parts, turned = refs
    depth, width = blocks[0].shape
    copies = []
    for n, (up, other) in enumerate(places):
        block = 2 * ((at_ref[1] + up) % 8) + (at_ref[2] + other) % 2
        cols = pl.ds(pl.multiple_of(block * depth, depth), depth)
        copies.append(pltpu.make_async_copy(a_ref.at[:, cols], held.at[n], sems.at[n]))
        copies[-1].start()
    for n, block in enumerate(blocks):
        hi, lo = parts_of(block[...], 2)
        for m, part in enumerate((hi, hi, lo)):
            b_parts[(3 * n + m) * depth:(3 * n + m + 1) * depth, :] = part
    for n, copy in enumerate(copies):
        copy.wait()
        hi, lo = parts_of(held[n], 2)
        for m, part in enumerate((hi, lo, hi)):
            a_parts[:, (3 * n + m) * depth:(3 * n + m + 1) * depth] = part
    tile = 256
    for m in range(held.shape[1] // tile):
        rows = slice(m * tile, (m + 1) * tile)
        for n in range(width // tile):
            cols = slice(n * tile, (n + 1) * tile)
            total = jnp.dot(a_parts[rows, :], b_parts[:, cols], preferred_element_type=F32)
            if has_total:
                total += before[rows, cols]
            if last:
                turned[cols, rows] = total.T
            else:
                outs[0][rows, cols] = total
    if last:
        for r in range(4):
            first = ((at_ref[0] + r) % 4) * 32
            for p in range(4):
                outs[r + p // 2 * 4][p % 2 * 32:p % 2 * 32 + 32, :] = turned[pl.ds(pl.multiple_of(p * 128 + first, 32), 32), :]


def sum_body(a, b, c, d, o):
    o[...] = (a[...] + b[...]) + (c[...] + d[...])


def pair_body(cuts, a, b, o, *sends):
    value = a[...] - b[...]
    o[...] = value
    for (first, count), ref in zip(cuts, sends):
        ref[...] = value[first:first + count, :]


def expand_body(quad_ref, table_ref, *refs):
    *ins, o_ref, held = refs
    at = 0
    for ref in ins:
        held[at:at + ref.shape[0], :] = ref[...]
        at += ref.shape[0]
    held[at:, :] = jnp.zeros((held.shape[0] - at, held.shape[1]), F32)
    row = lax.broadcasted_iota(jnp.int32, (held.shape[0], o_ref.shape[1]), 0)
    table = table_ref[quad_ref[0]]
    hot = jnp.where(row == table[0:1, :], table[1:2, :].astype(F32), 0.0).astype(BF16)
    turned = held[...].T
    acc = None
    for part in parts_of(turned, 3):
        term = jnp.dot(part, hot, preferred_element_type=F32)
        acc = term if acc is None else acc + term
    o_ref[...] = acc


def moved_along(value, axis, step):
    n = lax.axis_size(axis)
    return lax.ppermute(value, axis, [(k, (k + step) % n) for k in range(n)])


def flipped(value, axes, mask):
    n = lax.axis_size(axes)
    return lax.ppermute(value, axes, [(k, k ^ mask) for k in range(n)])


STEPS = (
    ((0, 0), (0, 0), (0, 0)),
    ((-1, 0), (1, 0), (1, 0)),
    ((-2, 0), (2, 0), (2, 0)),
    ((-3, 0), (2, 1), (-2, 0)),
    ((-2, 1), (3, 1), (-1, 0)),
)


def gather_step(held, step):
    up, down, across = STEPS[step]
    held[up[0] - 1, up[1]] = moved_along(held[up], "z", 1)
    held[down[0] + 1, down[1]] = moved_along(held[down], "z", -1)
    held[across[0], 1] = flipped(held[across], "xh", 1)
    return (up[0] - 1, up[1]), (down[0] + 1, down[1]), (across[0], 1)


def shards(integrals, amplitudes):
    xl, c, z, xh, y = (lax.axis_index(n) for n in ("xl", "c", "z", "xh", "y"))
    occ = 2 * xl + c
    quad = (4 * occ + y)[None]
    at = jnp.stack([y, z, xh])

    k = amplitudes.shape[0]
    kept, sent1, sent2, sent3 = call(
        select_body, [f32(k, 512), f32(k, 128), f32(k, 128), f32(k, 128)],
        occ[None], jnp.asarray(select_table()), amplitudes, smem=(0,))
    arrived = [flipped(value, ("xl", "c"), p) for p, value in ((1, sent1), (2, sent2), (3, sent3))]
    (unique,) = call(sub_body, [f32(k, 512)], kept, *arrived)

    def product(held, places, total, last):
        n = len(places)
        args = (at, integrals, *[held[p] for p in places]) + ((total,) if total is not None else ())
        out = [f32(64, 512)] * 8 if last else [f32(512, 512), f32(8, 128)]
        return call(functools.partial(product_body, places, total is not None, last), out, *args, smem=(0,), anywhere=(1,),
                    scratch=[pltpu.VMEM((n, 512, k), F32), pltpu.SemaphoreType.DMA((n,)), pltpu.VMEM((512, 3 * n * k), BF16),
                             pltpu.VMEM((3 * n * k, 512), BF16), pltpu.VMEM((512, 512), F32)],
                    vmem=VMEM_PRODUCT, flops=2 * 512 * n * k * 512 * 3)

    held = {(0, 0): unique}
    places, total = [(0, 0)], None
    turns, last = (), ()
    for step in range(5):
        if step:
            needed = list(dict.fromkeys(STEPS[step]))
            others = [held[p] for p in last if p not in needed]
            held.update(zip(needed, in_step(turns, *[held[p] for p in needed], after=others)))
        last = gather_step(held, step)
        if step:
            total, turn = product(held, tuple(places), total, False)
            turns = (turn,)
            places = []
        places += last
    total = product(held, tuple(places), total, True)

    perms = send_perms()
    pairs, arrived = [], []
    for n, pieces in enumerate((total[:4], total[4:])):
        moved = [moved_along(pieces[r], "y", r) for r in (1, 3, 2)]
        (mine,) = call(sum_body, [f32(64, 512)], pieces[0], *moved)
        lots = perms[4 * n:4 * n + 4]
        cuts = [(slots[0] - 64 * n, len(slots)) for slots, _ in lots]
        pair, *sends = call(functools.partial(pair_body, cuts), [f32(64, 512)] + [f32(count, 512) for _, count in cuts],
                            mine, moved_along(mine, "z", 4))
        pairs.append(pair)
        arrived += [lax.ppermute(value, GROUP, perm) for value, (_, perm) in zip(sends, lots)]
    (ladder,) = call(expand_body, [f32(512, 256)], quad, jnp.asarray(expand_table()), *pairs, *arrived,
                     scratch=[pltpu.VMEM((256, 512), F32)], smem=(0,))
    return ladder


def solution(mesh):
    fine = Mesh(mesh.devices.reshape(2, 2, 8, 2, 4), ("xl", "c", "z", "xh", "y"))
    in_specs = (P(("z", "xh"), "y"), P(("y", "z", "xh"), ("xl", "c")))
    out_specs = P(("z", "xh"), ("xl", "c", "y"))
    return jax.shard_map(shards, mesh=fine, in_specs=in_specs, out_specs=out_specs, check_vma=False)
```

```python
import functools

import jax
import jax.numpy as jnp
import numpy as np
from jax import lax
from jax.experimental import pallas as pl
from jax.experimental.pallas import tpu as pltpu
from jax.sharding import Mesh, PartitionSpec as P

O = 64
GROUP = ("xl", "c", "y")
F32, BF16 = jnp.float32, jnp.bfloat16
VMEM_PRODUCT = 50 * 2**20


def quad_partners(o, a, p):
    return (a, a ^ 2) if o < (o ^ p) else (a ^ 1, a ^ 3)


def own_pairs(o, a):
    g = 4 * o + a
    h = 4 * o + (a + 1) % 4
    out = [(4 * g + s, 4 * h + t) for s in range(4) for t in range(4)]
    h = 4 * o + (a ^ 2)
    if a < (a ^ 2):
        out += [(4 * g + s, 4 * h + t) for s in (0, 1) for t in range(4)]
    else:
        out += [(4 * g + s, 4 * h + t) for t in (2, 3) for s in range(4)]
    out += [(4 * g + s, 4 * g + t) for s in range(4) for t in range(s + 1, 4)]
    out += [None, None]
    lists = [out]
    for p in (1, 2, 3):
        lists.append([(4 * g + s, 4 * (4 * (o ^ p) + b) + t) for b in quad_partners(o, a, p) for s in range(4) for t in range(4)])
    return lists


def select_table():
    table = -np.ones((4, 2, 896), np.int32)
    for o in range(4):
        for a in range(4):
            for p, pairs in enumerate(own_pairs(o, a)):
                for k, pair in enumerate(pairs):
                    if pair is None:
                        continue
                    i, j = pair
                    at = p * 128 + a * 32 + k
                    table[o, 0, at] = (i - 16 * o) * O + j
                    if p == 0:
                        table[o, 1, at] = (j - 16 * o) * O + i
            for p in (1, 2, 3):
                for k, (j, i) in enumerate(own_pairs(o ^ p, a)[p]):
                    table[o, 0, 512 + (p - 1) * 128 + a * 32 + k] = (i - 16 * o) * O + j
    return table


def send_perms():
    quads = [(o, a) for o in range(4) for a in range(4)]
    perms = [
        (range(0, 16), [(4 * o + a, 4 * o + (a + 1) % 4) for o, a in quads]),
        (range(16, 24), [(4 * o + a, 4 * o + (a ^ 2)) for o, a in quads]),
    ]
    for p in (1, 2, 3):
        for t in (0, 1):
            start = 32 * p + 16 * t
            perms.append((range(start, start + 16), [(4 * o + a, 4 * (o ^ p) + quad_partners(o, a, p)[t]) for o, a in quads]))
    return perms


def expand_table():
    own = [sum(own_pairs(g // 4, g % 4), []) for g in range(16)]
    table = np.zeros((16, 2, 256), np.int32)
    table[:, 0] = -1
    held = [list(own[g]) for g in range(16)]
    for slots, perm in send_perms():
        for source, target in perm:
            held[target] += [own[source][s] for s in slots]
    for g in range(16):
        for slot, pair in enumerate(held[g]):
            if pair is None:
                continue
            for (i, j), sign in ((pair, 1), (pair[::-1], -1)):
                if i // 4 == g:
                    table[g, :, (i - 4 * g) * O + j] = slot, sign
        assert sum(table[g, 0] < 0) == 4
    return table


def parts_of(x, n):
    parts = []
    for _ in range(n):
        part = x.astype(BF16)
        parts.append(part)
        x = x - part.astype(F32)
    return parts


def call(body, out, *args, scratch=(), smem=(), vmem=16 * 2**20, anywhere=(), after=(), flops=0):
    spaces = [pltpu.SMEM if k in smem else pl.ANY if k in anywhere else pltpu.VMEM for k in range(len(args))]
    count = len(args)

    def without_after(*refs):
        body(*refs[:count], *refs[count + len(after):])

    return pl.pallas_call(
        without_after,
        out_shape=out,
        in_specs=[pl.BlockSpec(memory_space=m) for m in spaces + [pl.ANY] * len(after)],
        out_specs=[pl.BlockSpec(memory_space=pltpu.VMEM)] * len(out),
        scratch_shapes=list(scratch),
        compiler_params=pltpu.CompilerParams(vmem_limit_bytes=vmem),
        cost_estimate=pl.CostEstimate(flops=flops, bytes_accessed=0, transcendentals=0),
    )(*args, *after)


def in_step(turns, *arrays, after=()):
    count = len(arrays)

    def body(*refs):
        refs = refs[len(turns):]
        for source, target in zip(refs[:count], refs[count:]):
            target[...] = source[...]

    return call(body, [jax.ShapeDtypeStruct(a.shape, a.dtype) for a in arrays], *turns, *arrays, after=after)


def f32(*shape):
    return jax.ShapeDtypeStruct(shape, F32)


def select_body(occ_ref, table_ref, b_ref, *outs):
    kept, sent1, sent2, sent3 = outs
    parts = parts_of(b_ref[...], 2)
    for n, (ref, lo, p) in enumerate([
        (sent1, 0, 4), (sent2, 0, 5), (sent3, 0, 6), (kept, 0, 0), (kept, 128, 1), (kept, 256, 2), (kept, 384, 3)]):
        cols = slice(p * 128, p * 128 + 128)
        row = lax.broadcasted_iota(jnp.int32, (b_ref.shape[1], 128), 0)
        hot = jnp.where(row == table_ref[occ_ref[0], 0:1, cols], 1.0, 0.0)
        if p == 0:
            hot = hot - jnp.where(row == table_ref[occ_ref[0], 1:2, cols], 1.0, 0.0)
        hot = hot.astype(BF16)
        acc = jnp.dot(parts[0], hot, preferred_element_type=F32)
        for part in parts[1:]:
            acc += jnp.dot(part, hot, preferred_element_type=F32)
        ref[:, lo:lo + 128] = acc


def sub_body(x_ref, *refs):
    o_ref = refs[-1]
    width = x_ref.shape[1]
    first = width - 128 * (len(refs) - 1)
    if first:
        o_ref[:, :first] = x_ref[:, :first]
    for k, ref in enumerate(refs[:-1]):
        at = slice(first + 128 * k, first + 128 * k + 128)
        o_ref[:, at] = x_ref[:, at] - ref[...]


def product_body(places, has_total, last, at_ref, a_ref, *refs):
    refs = list(refs)
    blocks = [refs.pop(0) for _ in places]
    before = refs.pop(0) if has_total else None
    outs = [refs.pop(0) for _ in range(8 if last else 1)]
    if not last:
        turn = refs.pop(0)
        turn[...] = jnp.zeros_like(turn)
    held, sems, a_parts, b_parts, turned = refs
    depth, width = blocks[0].shape
    copies = []
    for n, (up, other) in enumerate(places):
        block = 2 * ((at_ref[1] + up) % 8) + (at_ref[2] + other) % 2
        cols = pl.ds(pl.multiple_of(block * depth, depth), depth)
        copies.append(pltpu.make_async_copy(a_ref.at[:, cols], held.at[n], sems.at[n]))
        copies[-1].start()
    for n, block in enumerate(blocks):
        hi, lo = parts_of(block[...], 2)
        for m, part in enumerate((hi, hi, lo)):
            b_parts[(3 * n + m) * depth:(3 * n + m + 1) * depth, :] = part
    for n, copy in enumerate(copies):
        copy.wait()
        hi, lo = parts_of(held[n], 2)
        for m, part in enumerate((hi, lo, hi)):
            a_parts[:, (3 * n + m) * depth:(3 * n + m + 1) * depth] = part
    tile = 256
    for m in range(held.shape[1] // tile):
        rows = slice(m * tile, (m + 1) * tile)
        for n in range(width // tile):
            cols = slice(n * tile, (n + 1) * tile)
            total = jnp.dot(a_parts[rows, :], b_parts[:, cols], preferred_element_type=F32)
            if has_total:
                total += before[rows, cols]
            if last:
                turned[cols, rows] = total.T
            else:
                outs[0][rows, cols] = total
    if last:
        for r in range(4):
            first = ((at_ref[0] + r) % 4) * 32
            for p in range(4):
                outs[r + p // 2 * 4][p % 2 * 32:p % 2 * 32 + 32, :] = turned[pl.ds(pl.multiple_of(p * 128 + first, 32), 32), :]


def sum_body(a, b, c, d, o):
    o[...] = (a[...] + b[...]) + (c[...] + d[...])


def pair_body(cuts, a, b, o, *sends):
    value = a[...] - b[...]
    o[...] = value
    for (first, count), ref in zip(cuts, sends):
        ref[...] = value[first:first + count, :]


def expand_body(quad_ref, table_ref, *refs):
    *ins, o_ref, held = refs
    at = 0
    for ref in ins:
        held[at:at + ref.shape[0], :] = ref[...]
        at += ref.shape[0]
    held[at:, :] = jnp.zeros((held.shape[0] - at, held.shape[1]), F32)
    row = lax.broadcasted_iota(jnp.int32, (held.shape[0], o_ref.shape[1]), 0)
    table = table_ref[quad_ref[0]]
    hot = jnp.where(row == table[0:1, :], table[1:2, :].astype(F32), 0.0).astype(BF16)
    turned = held[...].T
    acc = None
    for part in parts_of(turned, 2):
        term = jnp.dot(part, hot, preferred_element_type=F32)
        acc = term if acc is None else acc + term
    o_ref[...] = acc


def moved_along(value, axis, step):
    n = lax.axis_size(axis)
    return lax.ppermute(value, axis, [(k, (k + step) % n) for k in range(n)])


def flipped(value, axes, mask):
    n = lax.axis_size(axes)
    return lax.ppermute(value, axes, [(k, k ^ mask) for k in range(n)])


STEPS = (
    ((0, 0), (0, 0), (0, 0)),
    ((-1, 0), (1, 0), (1, 0)),
    ((-2, 0), (2, 0), (2, 0)),
    ((-3, 0), (2, 1), (-2, 0)),
    ((-2, 1), (3, 1), (-1, 0)),
)


def gather_step(held, step):
    up, down, across = STEPS[step]
    held[up[0] - 1, up[1]] = moved_along(held[up], "z", 1)
    held[down[0] + 1, down[1]] = moved_along(held[down], "z", -1)
    held[across[0], 1] = flipped(held[across], "xh", 1)
    return (up[0] - 1, up[1]), (down[0] + 1, down[1]), (across[0], 1)


def shards(integrals, amplitudes):
    xl, c, z, xh, y = (lax.axis_index(n) for n in ("xl", "c", "z", "xh", "y"))
    occ = 2 * xl + c
    quad = (4 * occ + y)[None]
    at = jnp.stack([y, z, xh])

    k = amplitudes.shape[0]
    kept, sent1, sent2, sent3 = call(
        select_body, [f32(k, 512), f32(k, 128), f32(k, 128), f32(k, 128)],
        occ[None], jnp.asarray(select_table()), amplitudes, smem=(0,))
    arrived = [flipped(value, ("xl", "c"), p) for p, value in ((1, sent1), (2, sent2), (3, sent3))]
    (unique,) = call(sub_body, [f32(k, 512)], kept, *arrived)

    def product(held, places, total, last):
        n = len(places)
        args = (at, integrals, *[held[p] for p in places]) + ((total,) if total is not None else ())
        out = [f32(64, 512)] * 8 if last else [f32(512, 512), f32(8, 128)]
        return call(functools.partial(product_body, places, total is not None, last), out, *args, smem=(0,), anywhere=(1,),
                    scratch=[pltpu.VMEM((n, 512, k), F32), pltpu.SemaphoreType.DMA((n,)), pltpu.VMEM((512, 3 * n * k), BF16),
                             pltpu.VMEM((3 * n * k, 512), BF16), pltpu.VMEM((512, 512), F32)],
                    vmem=VMEM_PRODUCT, flops=2 * 512 * n * k * 512 * 3)

    held = {(0, 0): unique}
    places, total = [(0, 0)], None
    turns, last = (), ()
    for step in range(5):
        if step:
            needed = list(dict.fromkeys(STEPS[step]))
            others = [held[p] for p in last if p not in needed]
            held.update(zip(needed, in_step(turns, *[held[p] for p in needed], after=others)))
        last = gather_step(held, step)
        if step:
            total, turn = product(held, tuple(places), total, False)
            turns = (turn,)
            places = []
        places += last
    total = product(held, tuple(places), total, True)

    perms = send_perms()
    pairs, arrived = [], []
    for n, pieces in enumerate((total[:4], total[4:])):
        moved = [moved_along(pieces[r], "y", r) for r in (1, 3, 2)]
        (mine,) = call(sum_body, [f32(64, 512)], pieces[0], *moved)
        lots = perms[4 * n:4 * n + 4]
        cuts = [(slots[0] - 64 * n, len(slots)) for slots, _ in lots]
        pair, *sends = call(functools.partial(pair_body, cuts), [f32(64, 512)] + [f32(count, 512) for _, count in cuts],
                            mine, moved_along(mine, "z", 4))
        pairs.append(pair)
        arrived += [lax.ppermute(value, GROUP, perm) for value, (_, perm) in zip(sends, lots)]
    (ladder,) = call(expand_body, [f32(512, 256)], quad, jnp.asarray(expand_table()), *pairs, *arrived,
                     scratch=[pltpu.VMEM((256, 512), F32)], smem=(0,))
    return ladder


def solution(mesh):
    fine = Mesh(mesh.devices.reshape(2, 2, 8, 2, 4), ("xl", "c", "z", "xh", "y"))
    in_specs = (P(("z", "xh"), "y"), P(("y", "z", "xh"), ("xl", "c")))
    out_specs = P(("z", "xh"), ("xl", "c", "y"))
    return jax.shard_map(shards, mesh=fine, in_specs=in_specs, out_specs=out_specs, check_vma=False)
```
